32 devices in a mesh: chan: 8 (over z, x), win: 4 (over y, core).
Axes of the slice: x: 2, y: 2, z: 4, core: 2. Of those that a mesh axis runs over, the one named last changes fastest.
Arguments:
- spectra: bfloat16 [2, 2, 2048, 4096], P(None, None, 'win', 'chan'), may hold values from -1000 to 1000
- near: int32 [8, 3], P('chan'), may hold values 0 or 1
Outputs:
- cross_spectra: float32 [4096, 4, 2, 2, 512], P(('chan', 'win'))
The draws below stay inside these ranges and needn't reach their ends.
All inputs are finite; a program needn't handle non-finite values. No bound on the sum of `near` on one device may be relied on, other than what follows from the above.
Results may differ from the reference program's by a relative error of at most 0.014.
Values may be sent and summed in bfloat16 or wider, within the bound.
A program may use at most 64 MiB of HBM per device.

```python
import math
import jax
import jax.numpy as jnp
from jax import lax

STA = 512
F = 2
WIN_DEV = 512
ROUNDS = 3
BLOCKS = 8
STATIONS = 4096
WINDOWS = 2048
N_WIN = 4


def draw_spectra(key, part):
    key = jax.random.fold_in(key, 11)
    first, second = jax.random.split(key, 2)
    shape = (2, F, WINDOWS, STATIONS)
    rising = jnp.exp(jnp.linspace(0.0, math.log(10.0), WINDOWS)).astype(jnp.float32)[None, None, :, None]
    base = jnp.clip(jax.random.normal(first, shape, jnp.float32), -6.0, 6.0)
    station = jnp.exp(jax.random.uniform(second, (1, F, 1, STATIONS), jnp.float32, 0.0, math.log(10.0)))
    return (base * station * rising).astype(jnp.bfloat16)


def place_ends(drawn, rng, low, top_value):
    dims = drawn.shape
    spot = [jax.random.randint(jax.random.fold_in(rng, axis), (), 0, dims[axis]) for axis in range(len(dims))]
    drawn = drawn.at[tuple(spot)].set(low)
    longest = dims.index(max(dims))
    spot[longest] = (spot[longest] + 1) % dims[longest]
    return drawn.at[tuple(spot)].set(top_value)


def setup_inputs(seed: int = 0) -> dict:
    key_of = jax.random.split(jax.random.key(seed), 3)
    spectra = draw_spectra(jax.random.fold_in(key_of[2], 71), 0)
    near = place_ends((jax.random.randint(key_of[1], (BLOCKS, ROUNDS), 0, 4) < 3).astype(jnp.int32), jax.random.fold_in(key_of[1], 1), 0, 1)
    return dict(spectra=spectra, near=near)


def cross_block(mine, other):
    width = mine.shape[-1]
    bins = []
    for f in range(F):
        left = jnp.concatenate([mine[0, f], mine[1, f]], axis=-1)
        right = jnp.concatenate([other[0, f], other[1, f]], axis=-1)
        product = jnp.dot(left.T, right, preferred_element_type=jnp.float32)
        real = product[:width, :width] + product[width:, width:]
        imag = product[:width, width:] - product[width:, :width]
        bins.append(jnp.stack([real, imag], axis=1))
    return jnp.stack(bins, axis=2)

def reference(spectra, near):
    blocks = jnp.transpose(spectra.reshape(2, F, WINDOWS, BLOCKS, STA), (3, 0, 1, 2, 4))

    def whiten(block):
        wide = block.astype(jnp.float32)
        energy = lax.optimization_barrier(jnp.sum(wide[0] * wide[0] + wide[1] * wide[1], axis=1))
        scale = lax.rsqrt(energy / WINDOWS + 1e-06)
        return (wide * scale[None, :, None, :]).astype(jnp.bfloat16)
    whitened = lax.map(whiten, blocks)

    def one_block(index):
        mine = whitened[index]
        rounds = []
        for r in range(ROUNDS + 1):
            source = jnp.maximum(index - r, 0)
            valid = (index - r >= 0).astype(jnp.bfloat16)
            other = whitened[source] * valid
            if r == 0:
                factor = jnp.float32(1.0)
            else:
                factor = near[index, r - 1].astype(jnp.float32)
            total = jnp.zeros((STA, 2, F, STA), jnp.float32)
            for g in range(N_WIN):
                part = cross_block(mine[:, :, g * WIN_DEV:(g + 1) * WIN_DEV, :], other[:, :, g * WIN_DEV:(g + 1) * WIN_DEV, :])
                rounded = lax.optimization_barrier((part * factor).astype(jnp.bfloat16))
                total = total + rounded.astype(jnp.float32)
            rounds.append(total * (1.0 / WINDOWS))
        return jnp.stack(rounds, axis=1)
    result = lax.map(one_block, jnp.arange(BLOCKS, dtype=jnp.int32))
    return result.reshape(STATIONS, ROUNDS + 1, 2, F, STA)
```

```python
import functools

import jax
import jax.numpy as jnp
from jax import lax
from jax.experimental import pallas as pl
from jax.experimental.pallas import tpu as pltpu
from jax.sharding import PartitionSpec as P

MESH = pl.DeviceIdType.MESH
LIFT = 2.0**40
EPS = 1e-06


def kernel(n_chan, n_win, windows, x_ref, near_ref, out_ref, blk, left, own, cs, cr, ys, yr, xs, xr,
           es, er, scale, column, bx_s, bx_r, bz_s, bz_r, c_s, c_r, y_s, y_r, r_s, r_r, e_s, e_r):
    depth, width = x_ref.shape[2], x_ref.shape[3]
    rows = width // n_win
    n_y = n_win // 2
    chan, win = lax.axis_index("chan"), lax.axis_index("win")
    p, pair = lax.rem(chan, 2), chan // 2
    core, y = lax.rem(win, 2), win // 2
    has_up = pair < n_chan // 2 - 1
    has_down = pair >= 1
    has_down2 = pair >= 2
    mate = (chan + 1 - 2 * p, win)
    up, down = (chan + 2, win), (chan - 2, win)
    twin = (chan, win + 1 - 2 * core)

    def win_peer(d):
        return (chan, lax.rem(win + d, n_win))

    def y_peer(d):
        return lax.rem(y + d, n_y)

    def remote(src, dst, ss, rs, to):
        return pltpu.make_async_remote_copy(
            src_ref=src, dst_ref=dst, send_sem=ss, recv_sem=rs, device_id=to, device_id_type=MESH)

    def exchange():
        return remote(x_ref.at[:, 1 - p], blk.at[p], bx_s, bx_r, mate)

    def exchanged():
        return remote(x_ref.at[:, p], blk.at[1 - p], bx_s, bx_r, mate)

    def climb(src, dst, n):
        return remote(blk.at[src], blk.at[dst], bz_s.at[n], bz_r.at[n], up)

    def core_copy(k):
        return remote(cs.at[k], cr.at[k], c_s.at[k], c_r.at[k], twin)

    def y_copy(k, d):
        return remote(ys.at[k, d - 1], yr.at[k, d - 1], y_s.at[k, d - 1], y_r.at[k, d - 1],
                      (chan, y_peer(d) * 2 + core))

    def result_copy(r):
        return remote(xs.at[r], xr.at[r], r_s.at[r], r_r.at[r], mate)

    def energy_copy(s, d):
        return remote(es.at[s], er.at[s, d - 1], e_s.at[s, d - 1], e_r.at[s, d - 1], win_peer(d))

    barrier = pltpu.get_barrier_semaphore()

    def greet(to):
        pl.semaphore_signal(barrier, inc=1, device_id=to, device_id_type=MESH)

    greet(mate)
    for d in range(1, n_win):
        greet(win_peer(d))
    pl.when(has_up)(lambda: greet(up))
    pl.when(has_down)(lambda: greet(down))
    pl.semaphore_wait(barrier, n_win + has_up.astype(jnp.int32) + has_down.astype(jnp.int32))

    exchange().start()
    blk[p] = x_ref[:, p]
    pl.when(has_up)(lambda: climb(p, 2 + p, 0).start())

    def energy(s):
        def step(i, total):
            part = blk[s, :, pl.ds(pl.multiple_of(i * 64, 64), 64)].astype(jnp.float32)
            return total + jnp.sum((part * part).reshape(2 * 8, 8, width), axis=0)

        total = lax.fori_loop(0, depth // 64, step, jnp.zeros((8, width), jnp.float32))
        es[s] = jnp.broadcast_to(jnp.sum(total, axis=0, keepdims=True), (8, width))
        for d in range(1, n_win):
            energy_copy(s, d).start()

    def finish_energy(s):
        total = es[s]
        for d in range(1, n_win):
            energy_copy(s, d).wait_recv()
            total = total + er[s, d - 1]
        scale[s] = lax.rsqrt(total / windows + EPS)

    def finish_column(kb):
        row = lax.broadcasted_iota(jnp.int32, (rows, width), 0) + win * rows
        lane = lax.broadcasted_iota(jnp.int32, (rows, width), 1)
        wide = jnp.broadcast_to(scale[kb, 0:1], (rows, width))
        picked = jnp.sum(jnp.where(row == lane, wide, 0.0), axis=1, keepdims=True)
        column[kb] = jnp.broadcast_to(picked * (1.0 / (LIFT * windows)), (rows, 128))

    def build_left(kb):
        lift = jnp.asarray(LIFT, jnp.bfloat16)
        real = (blk[kb, 0] * lift).T
        imag = (blk[kb, 1] * lift).T
        for q in range(n_win):
            base = ((q % 2) * n_y + q // 2) * 2 * rows
            cut = slice(q * rows, (q + 1) * rows)
            left[kb, base:base + rows, :depth] = real[cut]
            left[kb, base:base + rows, depth:] = imag[cut]
            left[kb, base + rows:base + 2 * rows, :depth] = -imag[cut]
            left[kb, base + rows:base + 2 * rows, depth:] = real[cut]

    def product(kb, r, s):
        k = kb * 4 + r
        right = blk[s].reshape(2 * depth, width)
        far = pl.multiple_of((1 - core) * width, width)
        near_by = pl.multiple_of(core * width, width)
        cs[k] = jnp.dot(left[kb, pl.ds(far, width)], right, preferred_element_type=jnp.float32).astype(jnp.bfloat16)
        core_copy(k).start()
        own[k] = jnp.dot(left[kb, pl.ds(near_by, width)], right, preferred_element_type=jnp.float32)

    def fold(kb, r, s):
        k = kb * 4 + r
        core_copy(k).wait_recv()
        for d in range(1, n_y):
            cut = pl.ds(pl.multiple_of(y_peer(d) * 2 * rows, 2 * rows), 2 * rows)
            ys[k, d - 1] = (own[k, cut] + cr[k, cut].astype(jnp.float32)).astype(jnp.bfloat16)
            y_copy(k, d).start()

    def weight(r):
        value = near_ref[0, jnp.maximum(r - 1, 0)]
        return jnp.where(r == 0, 1.0, value.astype(jnp.float32))

    def final(kb, r, s):
        k = kb * 4 + r
        cut = pl.ds(pl.multiple_of(y * 2 * rows, 2 * rows), 2 * rows)
        total = own[k, cut] + cr[k, cut].astype(jnp.float32)
        for d in range(1, n_y):
            y_copy(k, d).wait_recv()
            total = total + yr[k, d - 1].astype(jnp.float32)
        col = column[kb][:, 0:1]
        total = total.reshape(2, rows, width) * (col * scale[s, 0:1])[None]

        @pl.when(kb == p)
        def _():
            out_ref[r, :, p] = total * weight(r)

        @pl.when(kb != p)
        def _():
            xs[r] = total.astype(jnp.bfloat16)
            result_copy(r).start()

    groups = (
        (1, lambda n: (p, 0 * n, p)),
        (2, lambda n: (1 - p + n * p, n, (1 - p) * (1 - n))),
        (2, lambda n: (n, 2 - p + n, 2 + p)),
        (2, lambda n: (n, 1 + p + n, 3 - p)),
        (1, lambda n: (0 * n, 0 * n + 3, 0 * n + 4)),
    )

    def each(work, g):
        count, params = groups[g]

        def step(n, carry):
            work(*params(n))
            return carry

        lax.fori_loop(0, count, step, 0)

    energy(p)
    build_left(p)
    each(product, 0)
    exchanged().wait_recv()
    pl.when(has_up)(lambda: climb(1 - p, 3 - p, 1).start())
    build_left(1 - p)
    each(product, 1)
    each(fold, 0)
    each(fold, 1)
    energy(1 - p)

    @pl.when(has_down)
    def _():
        climb(p, 2 + p, 0).wait_recv()
        each(product, 2)
        each(fold, 2)
        energy(2 + p)

    for s in range(2):
        finish_energy(s)
        finish_column(s)
    each(final, 0)
    each(final, 1)

    @pl.when(has_down)
    def _():
        climb(1 - p, 3 - p, 1).wait_recv()
        pl.when(has_up)(lambda: climb(3, 4, 2).start())
        each(product, 3)
        each(fold, 3)
        energy(3 - p)
        finish_energy(2)
        finish_energy(3)
        each(final, 2)

    @pl.when(has_down2)
    def _():
        climb(3, 4, 2).wait_recv()
        each(product, 4)
        each(fold, 4)
        energy(4)

    pl.when(has_down)(lambda: each(final, 3))

    @pl.when(has_down2)
    def _():
        finish_energy(4)
        each(final, 4)

    def receive(r, carry):
        @pl.when(chan >= r)
        def _():
            result_copy(r).wait_recv()
            out_ref[r, :, 1 - p] = xr[r].astype(jnp.float32) * weight(r)

        @pl.when(chan < r)
        def _():
            out_ref[r] = jnp.zeros(out_ref.shape[1:], jnp.float32)

        return carry

    lax.fori_loop(0, 4, receive, 0)

    exchange().wait_send()

    @pl.when(has_up)
    def _():
        climb(p, 2 + p, 0).wait_send()
        climb(1 - p, 3 - p, 1).wait_send()
        pl.when(has_down)(lambda: climb(3, 4, 2).wait_send())

    def sent(kb, r, s):
        core_copy(kb * 4 + r).wait_send()
        for d in range(1, n_y):
            y_copy(kb * 4 + r, d).wait_send()
        pl.when(kb != p)(lambda: result_copy(r).wait_send())

    def energy_sent(s):
        for d in range(1, n_win):
            energy_copy(s, d).wait_send()

    each(sent, 0)
    each(sent, 1)
    energy_sent(0)
    energy_sent(1)

    @pl.when(has_down)
    def _():
        each(sent, 2)
        each(sent, 3)
        energy_sent(2)
        energy_sent(3)

    @pl.when(has_down2)
    def _():
        each(sent, 4)
        energy_sent(4)


def on_device(n_chan, n_win, spectra, near):
    _, freqs, depth, width = spectra.shape
    rounds = near.shape[1] + 1
    rows, n_y = width // n_win, n_win // 2
    bf, f32 = jnp.bfloat16, jnp.float32
    dma = pltpu.SemaphoreType.DMA
    out = pl.pallas_call(
        functools.partial(kernel, n_chan, n_win, float(depth * n_win)),
        out_shape=jax.ShapeDtypeStruct((rounds, 2, freqs, rows, width), f32),
        in_specs=[pl.BlockSpec(memory_space=pltpu.VMEM), pl.BlockSpec(memory_space=pltpu.SMEM)],
        out_specs=pl.BlockSpec(memory_space=pltpu.VMEM),
        scratch_shapes=[
            pltpu.VMEM((5, 2, depth, width), bf),
            pltpu.VMEM((2, 2 * width, 2 * depth), bf),
            pltpu.VMEM((8, width, width), f32),
            pltpu.VMEM((8, width, width), bf),
            pltpu.VMEM((8, width, width), bf),
            pltpu.VMEM((8, n_y - 1, 2 * rows, width), bf),
            pltpu.VMEM((8, n_y - 1, 2 * rows, width), bf),
            pltpu.VMEM((rounds, 2, rows, width), bf),
            pltpu.VMEM((rounds, 2, rows, width), bf),
            pltpu.VMEM((5, 8, width), f32),
            pltpu.VMEM((5, n_win - 1, 8, width), f32),
            pltpu.VMEM((5, 8, width), f32),
            pltpu.VMEM((2, rows, 128), f32),
            dma, dma, dma((3,)), dma((3,)), dma((8,)), dma((8,)),
            dma((8, n_y - 1)), dma((8, n_y - 1)), dma((rounds,)), dma((rounds,)),
            dma((5, n_win - 1)), dma((5, n_win - 1)),
        ],
        compiler_params=pltpu.CompilerParams(
            collective_id=0, has_side_effects=True, vmem_limit_bytes=56 * 1024 * 1024),
        cost_estimate=pl.CostEstimate(
            flops=64 * depth * width * width, bytes_accessed=6 * 1024 * 1024, transcendentals=0),
    )(spectra, near)
    return jnp.transpose(out, (3, 0, 1, 2, 4))


def solution(mesh):
    sizes = dict(mesh.shape)
    return jax.shard_map(
        functools.partial(on_device, sizes["chan"], sizes["win"]),
        mesh=mesh,
        in_specs=(P(None, None, "win", "chan"), P("chan", None)),
        out_specs=P(("chan", "win"), None, None, None, None),
        check_vma=False,
    )
```

```python
import functools

import jax
import jax.numpy as jnp
from jax import lax
from jax.experimental import pallas as pl
from jax.experimental.pallas import tpu as pltpu
from jax.sharding import PartitionSpec as P

MESH = pl.DeviceIdType.MESH
LIFT = 2.0**40
EPS = 1e-06


def kernel(n_chan, n_win, windows, x_ref, near_ref, out_ref, blk, left, own, cs, cr, ys, yr, xs, xr,
           es, er, scale, column, bx_s, bx_r, bu_s, bu_r, bd_s, bd_r, c_s, c_r, y_s, y_r, r_s, r_r,
           e_s, e_r):
    depth, width = x_ref.shape[2], x_ref.shape[3]
    rows = width // n_win
    n_y = n_win // 2
    chan, win = lax.axis_index("chan"), lax.axis_index("win")
    p, pair = lax.rem(chan, 2), chan // 2
    core, y = lax.rem(win, 2), win // 2
    has_up = pair < n_chan // 2 - 1
    has_down = pair >= 1
    has_both = jnp.logical_and(has_up, has_down)
    even, odd = p == 0, p == 1
    mate = (chan + 1 - 2 * p, win)
    up, down = (chan + 2, win), (chan - 2, win)
    up_mate, down_mate = (chan + 3 - 2 * p, win), (chan - 1 - 2 * p, win)
    twin = (chan, win + 1 - 2 * core)

    def win_peer(d):
        return (chan, lax.rem(win + d, n_win))

    def y_peer(d):
        return lax.rem(y + d, n_y)

    def remote(src, dst, ss, rs, to):
        return pltpu.make_async_remote_copy(
            src_ref=src, dst_ref=dst, send_sem=ss, recv_sem=rs, device_id=to, device_id_type=MESH)

    def exchange(c):
        return remote(x_ref.at[c, 1 - p], blk.at[p, c], bx_s.at[c], bx_r.at[c], mate)

    def exchanged(c):
        return remote(x_ref.at[c, p], blk.at[1 - p, c], bx_s.at[c], bx_r.at[c], mate)

    def climb(c):
        return remote(blk.at[1, c], blk.at[2, c], bu_s.at[c], bu_r.at[c], up)

    def descend(slot, n):
        return remote(blk.at[slot], blk.at[3 + slot], bd_s.at[n], bd_r.at[n], down)

    def core_copy(k):
        return remote(cs.at[k], cr.at[k], c_s.at[k], c_r.at[k], twin)

    def y_copy(k, d):
        return remote(ys.at[k, d - 1], yr.at[k, d - 1], y_s.at[k, d - 1], y_r.at[k, d - 1],
                      (chan, y_peer(d) * 2 + core))

    def result_copy(m, r, w, to):
        return remote(xs.at[m], xr.at[r, w], r_s.at[m], r_r.at[r, w], to)

    def energy_copy(s, d):
        return remote(es.at[s], er.at[s, d - 1], e_s.at[s, d - 1], e_r.at[s, d - 1], win_peer(d))

    barrier = pltpu.get_barrier_semaphore()

    def greet(*others):
        for to in others:
            pl.semaphore_signal(barrier, inc=1, device_id=to, device_id_type=MESH)

    greet(mate)
    for d in range(1, n_win):
        greet(win_peer(d))
    pl.when(has_up)(lambda: greet(up, up_mate))
    pl.when(has_down)(lambda: greet(down, down_mate))
    pl.semaphore_wait(barrier, n_win + 2 * (has_up.astype(jnp.int32) + has_down.astype(jnp.int32)))

    for c in range(2):
        exchange(c).start()
    blk[p] = x_ref[:, p]

    @pl.when(has_down)
    def _():
        descend(p, 0).start()

    @pl.when(jnp.logical_and(has_up, odd))
    def _():
        for c in range(2):
            climb(c).start()

    def energy(s):
        def step(i, total):
            part = blk[s, :, pl.ds(pl.multiple_of(i * 64, 64), 64)].astype(jnp.float32)
            return total + jnp.sum((part * part).reshape(2 * 8, 8, width), axis=0)

        total = lax.fori_loop(0, depth // 64, step, jnp.zeros((8, width), jnp.float32))
        es[s] = jnp.broadcast_to(jnp.sum(total, axis=0, keepdims=True), (8, width))
        for d in range(1, n_win):
            energy_copy(s, d).start()

    def finish_energy(s):
        total = es[s]
        for d in range(1, n_win):
            energy_copy(s, d).wait_recv()
            total = total + er[s, d - 1]
        scale[s] = lax.rsqrt(total / windows + EPS)

    def finish_column(kb, s):
        row = lax.broadcasted_iota(jnp.int32, (rows, width), 0) + win * rows
        lane = lax.broadcasted_iota(jnp.int32, (rows, width), 1)
        wide = jnp.broadcast_to(scale[s, 0:1], (rows, width))
        picked = jnp.sum(jnp.where(row == lane, wide, 0.0), axis=1, keepdims=True)
        column[kb] = jnp.broadcast_to(picked * (1.0 / (LIFT * windows)), (rows, 128))

    def build_left(kb, s):
        lift = jnp.asarray(LIFT, jnp.bfloat16)
        real = (blk[s, 0] * lift).T
        imag = (blk[s, 1] * lift).T
        for q in range(n_win):
            base = ((q % 2) * n_y + q // 2) * 2 * rows
            cut = slice(q * rows, (q + 1) * rows)
            left[kb, base:base + rows, :depth] = real[cut]
            left[kb, base:base + rows, depth:] = imag[cut]
            left[kb, base + rows:base + 2 * rows, :depth] = -imag[cut]
            left[kb, base + rows:base + 2 * rows, depth:] = real[cut]

    def product(m, kb, s, q, r):
        right = blk[s].reshape(2 * depth, width)
        far = pl.multiple_of((1 - core) * width, width)
        near_by = pl.multiple_of(core * width, width)
        cs[m] = jnp.dot(left[kb, pl.ds(far, width)], right, preferred_element_type=jnp.float32).astype(jnp.bfloat16)
        core_copy(m).start()
        own[m] = jnp.dot(left[kb, pl.ds(near_by, width)], right, preferred_element_type=jnp.float32)

    def fold(m, kb, s, q, r):
        core_copy(m).wait_recv()
        for d in range(1, n_y):
            cut = pl.ds(pl.multiple_of(y_peer(d) * 2 * rows, 2 * rows), 2 * rows)
            ys[m, d - 1] = (own[m, cut] + cr[m, cut].astype(jnp.float32)).astype(jnp.bfloat16)
            y_copy(m, d).start()

    def weight(r):
        value = near_ref[0, jnp.maximum(r - 1, 0)]
        return jnp.where(r == 0, 1.0, value.astype(jnp.float32))

    def store(r, f, value):
        out_ref[r, :, f] = value * weight(r)

    def total_of(m, kb, s):
        cut = pl.ds(pl.multiple_of(y * 2 * rows, 2 * rows), 2 * rows)
        total = own[m, cut] + cr[m, cut].astype(jnp.float32)
        for d in range(1, n_y):
            y_copy(m, d).wait_recv()
            total = total + yr[m, d - 1].astype(jnp.float32)
        return total.reshape(2, rows, width) * (column[kb][:, 0:1] * scale[s, 0:1])[None]

    def final_here(m, kb, s, q, r):
        total = total_of(m, kb, s)

        @pl.when(q == p)
        def _():
            store(r, p, total)

        @pl.when(q != p)
        def _():
            xs[m] = total.astype(jnp.bfloat16)
            result_copy(m, r, 0, mate).start()

    def target_up(m, r, q):
        same = (q == p).astype(jnp.int32)
        return result_copy(m, r, same, (chan - p + 2 + q, win))

    def final_up(m, kb, s, q, r):
        xs[m] = total_of(m, kb, s).astype(jnp.bfloat16)
        target_up(m, r, q).start()

    groups = dict(
        mine=(1, lambda n: (p, p, p, p, 0 * n)),
        pair=(2, lambda n: (1 - p + n * (1 + p), 1 - p + n * p, (1 - p) * (1 - n), 1 - p + n * p, n)),
        above=(1, lambda n: (5 + p + 0 * n, 2 + p, 0 * n, p, 2 + p)),
        below=(2, lambda n: (3 + n, n, 0 * n + 2, n, 1 + n)),
        other=(1, lambda n: (6 - p + 0 * n, 3 - p, 0 * n, 1 - p, 3 - p)),
        span=(1, lambda n: (0 * n + 7, 0 * n + 2, 0 * n + 2, 0 * n, 0 * n + 3)),
    )

    def each(work, g):
        count, params = groups[g]

        def step(n, carry):
            work(*params(n))
            return carry

        lax.fori_loop(0, count, step, 0)

    def make(g):
        each(product, g)
        each(fold, g)

    build_left(p, p)
    each(product, "mine")
    energy(p)
    each(fold, "mine")
    for c in range(2):
        exchanged(c).wait_recv()
        pl.when(jnp.logical_and(has_up, even))(lambda: climb(c).start())
    pl.when(has_down)(lambda: descend(1 - p, 1).start())
    build_left(1 - p, 1 - p)
    make("pair")
    energy(1 - p)

    @pl.when(has_up)
    def _():
        descend(p, 0).wait_recv()
        build_left(2 + p, 3 + p)
        make("above")
        energy(3 + p)

    for s in range(2):
        finish_energy(s)
        finish_column(s, s)
    each(final_here, "mine")

    @pl.when(has_down)
    def _():
        for c in range(2):
            climb(c).wait_recv()
        make("below")
        energy(2)

    pl.when(jnp.logical_and(has_both, even))(lambda: make("span"))
    each(final_here, "pair")

    @pl.when(has_up)
    def _():
        finish_energy(3 + p)
        finish_column(2 + p, 3 + p)
        each(final_up, "above")
        descend(1 - p, 1).wait_recv()
        build_left(3 - p, 4 - p)
        make("other")
        energy(4 - p)

    pl.when(jnp.logical_and(has_both, odd))(lambda: make("span"))

    @pl.when(has_down)
    def _():
        finish_energy(2)
        each(final_here, "below")

    @pl.when(has_up)
    def _():
        finish_energy(4 - p)
        finish_column(3 - p, 4 - p)
        each(final_up, "other")

    pl.when(has_both)(lambda: each(final_up, "span"))

    def receive(r, carry):
        @pl.when(chan >= r)
        def _():
            result_copy(0, r, 0, mate).wait_recv()
            store(r, 1 - p, xr[r, 0].astype(jnp.float32).reshape(2, rows, width))

        @pl.when(jnp.logical_and(chan >= r, r >= 2 + p))
        def _():
            result_copy(0, r, 1, mate).wait_recv()
            store(r, p, xr[r, 1].astype(jnp.float32).reshape(2, rows, width))

        @pl.when(chan < r)
        def _():
            out_ref[r] = jnp.zeros(out_ref.shape[1:], jnp.float32)

        return carry

    lax.fori_loop(0, 4, receive, 0)

    for c in range(2):
        exchange(c).wait_send()

    @pl.when(has_up)
    def _():
        for c in range(2):
            climb(c).wait_send()

    @pl.when(has_down)
    def _():
        descend(p, 0).wait_send()
        descend(1 - p, 1).wait_send()

    def sent(m, kb, s, q, r):
        core_copy(m).wait_send()
        for d in range(1, n_y):
            y_copy(m, d).wait_send()

    def sent_here(m, kb, s, q, r):
        sent(m, kb, s, q, r)
        pl.when(q != p)(lambda: result_copy(m, r, 0, mate).wait_send())

    def sent_up(m, kb, s, q, r):
        sent(m, kb, s, q, r)
        target_up(m, r, q).wait_send()

    def energy_sent(s):
        for d in range(1, n_win):
            energy_copy(s, d).wait_send()

    each(sent_here, "mine")
    each(sent_here, "pair")
    energy_sent(0)
    energy_sent(1)

    @pl.when(has_down)
    def _():
        each(sent_here, "below")
        energy_sent(2)

    @pl.when(has_up)
    def _():
        each(sent_up, "above")
        each(sent_up, "other")
        energy_sent(3)
        energy_sent(4)

    pl.when(has_both)(lambda: each(sent_up, "span"))


def on_device(n_chan, n_win, spectra, near):
    _, freqs, depth, width = spectra.shape
    rounds = near.shape[1] + 1
    rows, n_y = width // n_win, n_win // 2
    bf, f32 = jnp.bfloat16, jnp.float32
    dma = pltpu.SemaphoreType.DMA
    out = pl.pallas_call(
        functools.partial(kernel, n_chan, n_win, float(depth * n_win)),
        out_shape=jax.ShapeDtypeStruct((rounds, 2, freqs, rows, width), f32),
        in_specs=[pl.BlockSpec(memory_space=pltpu.VMEM), pl.BlockSpec(memory_space=pltpu.SMEM)],
        out_specs=pl.BlockSpec(memory_space=pltpu.VMEM),
        scratch_shapes=[
            pltpu.VMEM((5, 2, depth, width), bf),
            pltpu.VMEM((4, 2 * width, 2 * depth), bf),
            pltpu.VMEM((8, width, width), f32),
            pltpu.VMEM((8, width, width), bf),
            pltpu.VMEM((8, width, width), bf),
            pltpu.VMEM((8, n_y - 1, 2 * rows, width), bf),
            pltpu.VMEM((8, n_y - 1, 2 * rows, width), bf),
            pltpu.VMEM((8, 2, rows, width), bf),
            pltpu.VMEM((rounds, 2, 2, rows, width), bf),
            pltpu.VMEM((5, 8, width), f32),
            pltpu.VMEM((5, n_win - 1, 8, width), f32),
            pltpu.VMEM((5, 8, width), f32),
            pltpu.VMEM((4, rows, 128), f32),
            dma((2,)), dma((2,)), dma((2,)), dma((2,)), dma((2,)), dma((2,)), dma((8,)), dma((8,)),
            dma((8, n_y - 1)), dma((8, n_y - 1)), dma((8,)), dma((rounds, 2)),
            dma((5, n_win - 1)), dma((5, n_win - 1)),
        ],
        compiler_params=pltpu.CompilerParams(
            collective_id=0, has_side_effects=True, vmem_limit_bytes=56 * 1024 * 1024),
        cost_estimate=pl.CostEstimate(
            flops=64 * depth * width * width, bytes_accessed=6 * 1024 * 1024, transcendentals=0),
    )(spectra, near)
    return jnp.transpose(out, (3, 0, 1, 2, 4))


def solution(mesh):
    sizes = dict(mesh.shape)
    return jax.shard_map(
        functools.partial(on_device, sizes["chan"], sizes["win"]),
        mesh=mesh,
        in_specs=(P(None, None, "win", "chan"), P("chan", None)),
        out_specs=P(("chan", "win"), None, None, None, None),
        check_vma=False,
    )
```

```python
import functools

import jax
import jax.numpy as jnp
from jax import lax
from jax.experimental import pallas as pl
from jax.experimental.pallas import tpu as pltpu
from jax.sharding import PartitionSpec as P

MESH = pl.DeviceIdType.MESH
LIFT = 2.0**40
EPS = 1e-06


def kernel(n_chan, n_win, windows, x_ref, near_ref, out_ref, blk, left, own, cs, cr, ys, yr, xs, xr,
           es, er, scale, column, bx_s, bx_r, bu_s, bu_r, bd_s, bd_r, c_s, c_r, y_s, y_r, r_s, r_r,
           e_s, e_r):
    depth, width = x_ref.shape[2], x_ref.shape[3]
    rows = width // n_win
    n_y = n_win // 2
    step_rows = out_ref.shape[0] // rows
    chan, win = lax.axis_index("chan"), lax.axis_index("win")
    p, pair = lax.rem(chan, 2), chan // 2
    core, y = lax.rem(win, 2), win // 2
    has_up = pair < n_chan // 2 - 1
    has_down = pair >= 1
    has_both = jnp.logical_and(has_up, has_down)
    even, odd = p == 0, p == 1
    mate = (chan + 1 - 2 * p, win)
    up, down = (chan + 2, win), (chan - 2, win)
    up_mate, down_mate = (chan + 3 - 2 * p, win), (chan - 1 - 2 * p, win)
    twin = (chan, win + 1 - 2 * core)

    def win_peer(d):
        return (chan, lax.rem(win + d, n_win))

    def y_peer(d):
        return lax.rem(y + d, n_y)

    def remote(src, dst, ss, rs, to):
        return pltpu.make_async_remote_copy(
            src_ref=src, dst_ref=dst, send_sem=ss, recv_sem=rs, device_id=to, device_id_type=MESH)

    def exchange(c):
        return remote(x_ref.at[c, 1 - p], blk.at[p, c], bx_s.at[c], bx_r.at[c], mate)

    def exchanged(c):
        return remote(x_ref.at[c, p], blk.at[1 - p, c], bx_s.at[c], bx_r.at[c], mate)

    def climb(c):
        return remote(blk.at[1, c], blk.at[2, c], bu_s.at[c], bu_r.at[c], up)

    def descend(slot, n):
        return remote(blk.at[slot], blk.at[3 + slot], bd_s.at[n], bd_r.at[n], down)

    def core_copy(k):
        return remote(cs.at[k], cr.at[k], c_s.at[k], c_r.at[k], twin)

    def y_copy(k, d):
        return remote(ys.at[k, d - 1], yr.at[k, d - 1], y_s.at[k, d - 1], y_r.at[k, d - 1],
                      (chan, y_peer(d) * 2 + core))

    def result_copy(m, r, w, to):
        return remote(xs.at[m], xr.at[r, w], r_s.at[m], r_r.at[r, w], to)

    def energy_copy(s, d):
        return remote(es.at[s], er.at[s, d - 1], e_s.at[s, d - 1], e_r.at[s, d - 1], win_peer(d))

    barrier = pltpu.get_barrier_semaphore()

    def greet(*others):
        for to in others:
            pl.semaphore_signal(barrier, inc=1, device_id=to, device_id_type=MESH)

    greet(mate)
    for d in range(1, n_win):
        greet(win_peer(d))
    pl.when(has_up)(lambda: greet(up, up_mate))
    pl.when(has_down)(lambda: greet(down, down_mate))
    pl.semaphore_wait(barrier, n_win + 2 * (has_up.astype(jnp.int32) + has_down.astype(jnp.int32)))

    for c in range(2):
        exchange(c).start()
    blk[p] = x_ref[:, p]

    @pl.when(has_down)
    def _():
        descend(p, 0).start()

    @pl.when(jnp.logical_and(has_up, odd))
    def _():
        for c in range(2):
            climb(c).start()

    def energy(s):
        def step(i, total):
            part = blk[s, :, pl.ds(pl.multiple_of(i * 64, 64), 64)].astype(jnp.float32)
            return total + jnp.sum((part * part).reshape(2 * 8, 8, width), axis=0)

        total = lax.fori_loop(0, depth // 64, step, jnp.zeros((8, width), jnp.float32))
        es[s] = jnp.broadcast_to(jnp.sum(total, axis=0, keepdims=True), (8, width))
        for d in range(1, n_win):
            energy_copy(s, d).start()

    def finish_energy(s):
        total = es[s]
        for d in range(1, n_win):
            energy_copy(s, d).wait_recv()
            total = total + er[s, d - 1]
        scale[s] = lax.rsqrt(total / windows + EPS)

    def finish_column(kb, s):
        row = lax.broadcasted_iota(jnp.int32, (rows, width), 0) + win * rows
        lane = lax.broadcasted_iota(jnp.int32, (rows, width), 1)
        wide = jnp.broadcast_to(scale[s, 0:1], (rows, width))
        picked = jnp.sum(jnp.where(row == lane, wide, 0.0), axis=1, keepdims=True)
        column[kb] = jnp.broadcast_to(picked * (1.0 / (LIFT * windows)), (rows, 128))

    def build_left(kb, s):
        lift = jnp.asarray(LIFT, jnp.bfloat16)
        real = (blk[s, 0] * lift).T
        imag = (blk[s, 1] * lift).T
        for q in range(n_win):
            base = ((q % 2) * n_y + q // 2) * 2 * rows
            cut = slice(q * rows, (q + 1) * rows)
            left[kb, base:base + rows, :depth] = real[cut]
            left[kb, base:base + rows, depth:] = imag[cut]
            left[kb, base + rows:base + 2 * rows, :depth] = -imag[cut]
            left[kb, base + rows:base + 2 * rows, depth:] = real[cut]

    def product(m, kb, s, q, r):
        right = blk[s].reshape(2 * depth, width)
        far = pl.multiple_of((1 - core) * width, width)
        near_by = pl.multiple_of(core * width, width)
        cs[m] = jnp.dot(left[kb, pl.ds(far, width)], right, preferred_element_type=jnp.float32).astype(jnp.bfloat16)
        core_copy(m).start()
        own[m] = jnp.dot(left[kb, pl.ds(near_by, width)], right, preferred_element_type=jnp.float32)

    def fold(m, kb, s, q, r):
        core_copy(m).wait_recv()
        for d in range(1, n_y):
            cut = pl.ds(pl.multiple_of(y_peer(d) * 2 * rows, 2 * rows), 2 * rows)
            ys[m, d - 1] = (own[m, cut] + cr[m, cut].astype(jnp.float32)).astype(jnp.bfloat16)
            y_copy(m, d).start()

    def weight(r):
        value = near_ref[0, jnp.maximum(r - 1, 0)]
        return jnp.where(r == 0, 1.0, value.astype(jnp.float32))

    def store(r, f, value):
        value = value * weight(r)
        for c in range(2):
            for tile in range(width // 128):
                at = pl.ds(((r * 2 + c) * (width // 128) + tile) * 2 + f, rows, stride=step_rows)
                out_ref[at, :] = value[c, :, tile * 128:(tile + 1) * 128]

    def total_of(m, kb, s):
        cut = pl.ds(pl.multiple_of(y * 2 * rows, 2 * rows), 2 * rows)
        total = own[m, cut] + cr[m, cut].astype(jnp.float32)
        for d in range(1, n_y):
            y_copy(m, d).wait_recv()
            total = total + yr[m, d - 1].astype(jnp.float32)
        return total.reshape(2, rows, width) * (column[kb][:, 0:1] * scale[s, 0:1])[None]

    def final_here(m, kb, s, q, r):
        total = total_of(m, kb, s)

        @pl.when(q == p)
        def _():
            store(r, p, total)

        @pl.when(q != p)
        def _():
            xs[m] = total.astype(jnp.bfloat16)
            result_copy(m, r, 0, mate).start()

    def final_twist(m, kb, s, q, r):
        store(r, 1 - p, total_of(m, kb, s))

    def target_up(m, r, q):
        same = (q == p).astype(jnp.int32)
        return result_copy(m, r, same, (chan - p + 2 + q, win))

    def final_up(m, kb, s, q, r):
        xs[m] = total_of(m, kb, s).astype(jnp.bfloat16)
        target_up(m, r, q).start()

    groups = dict(
        mine=(1, lambda n: (0 * n, p, p, p, 0 * n)),
        twist=(1, lambda n: (0 * n + 1, 0 * n + 4, 0 * n + 5, p, 0 * n)),
        pair=(1, lambda n: (0 * n + 2, 0 * n + 1, 0 * n, 0 * n + 1, 0 * n + 1)),
        above=(1, lambda n: (5 + p + 0 * n, 2 + p, 0 * n, p, 2 + p)),
        below=(2, lambda n: (3 + n, n, 0 * n + 2, n, 1 + n)),
        other=(1, lambda n: (6 - p + 0 * n, 3 - p, 0 * n, 1 - p, 3 - p)),
        span=(1, lambda n: (0 * n + 7, 0 * n + 2, 0 * n + 2, 0 * n, 0 * n + 3)),
    )

    def each(work, g):
        count, params = groups[g]

        def step(n, carry):
            work(*params(n))
            return carry

        lax.fori_loop(0, count, step, 0)

    def make(g):
        each(product, g)
        each(fold, g)

    build_left(p, p)
    each(product, "mine")
    blk[5] = x_ref[:, 1 - p]
    build_left(4, 5)
    each(product, "twist")
    each(fold, "mine")
    each(fold, "twist")
    energy(p)
    energy(5)
    for c in range(2):
        exchanged(c).wait_recv()
        pl.when(jnp.logical_and(has_up, even))(lambda: climb(c).start())
    pl.when(has_down)(lambda: descend(1 - p, 1).start())
    build_left(1 - p, 1 - p)
    make("pair")
    energy(1 - p)

    @pl.when(has_up)
    def _():
        descend(p, 0).wait_recv()
        build_left(2 + p, 3 + p)
        make("above")
        energy(3 + p)

    for s in range(2):
        finish_energy(s)
        finish_column(s, s)
    finish_energy(5)
    finish_column(4, 5)
    each(final_here, "mine")
    each(final_twist, "twist")

    @pl.when(has_down)
    def _():
        for c in range(2):
            climb(c).wait_recv()
        make("below")
        energy(2)

    pl.when(jnp.logical_and(has_both, even))(lambda: make("span"))
    each(final_here, "pair")

    @pl.when(has_up)
    def _():
        finish_energy(3 + p)
        finish_column(2 + p, 3 + p)
        each(final_up, "above")
        descend(1 - p, 1).wait_recv()
        build_left(3 - p, 4 - p)
        make("other")
        energy(4 - p)

    pl.when(jnp.logical_and(has_both, odd))(lambda: make("span"))

    @pl.when(has_down)
    def _():
        finish_energy(2)
        each(final_here, "below")

    @pl.when(has_up)
    def _():
        finish_energy(4 - p)
        finish_column(3 - p, 4 - p)
        each(final_up, "other")

    pl.when(has_both)(lambda: each(final_up, "span"))

    def receive(r, carry):
        @pl.when(jnp.logical_and(chan >= r, r >= 1))
        def _():
            result_copy(0, r, 0, mate).wait_recv()
            store(r, 1 - p, xr[r, 0].astype(jnp.float32).reshape(2, rows, width))

        @pl.when(jnp.logical_and(chan >= r, r >= 2 + p))
        def _():
            result_copy(0, r, 1, mate).wait_recv()
            store(r, p, xr[r, 1].astype(jnp.float32).reshape(2, rows, width))

        @pl.when(chan < r)
        def _():
            for f in range(2):
                store(r, f, jnp.zeros((2, rows, width), jnp.float32))

        return carry

    lax.fori_loop(0, 4, receive, 0)

    for c in range(2):
        exchange(c).wait_send()

    @pl.when(has_up)
    def _():
        for c in range(2):
            climb(c).wait_send()

    @pl.when(has_down)
    def _():
        descend(p, 0).wait_send()
        descend(1 - p, 1).wait_send()

    def sent(m, kb, s, q, r):
        core_copy(m).wait_send()
        for d in range(1, n_y):
            y_copy(m, d).wait_send()

    def sent_here(m, kb, s, q, r):
        sent(m, kb, s, q, r)
        pl.when(q != p)(lambda: result_copy(m, r, 0, mate).wait_send())

    def sent_up(m, kb, s, q, r):
        sent(m, kb, s, q, r)
        target_up(m, r, q).wait_send()

    def energy_sent(s):
        for d in range(1, n_win):
            energy_copy(s, d).wait_send()

    each(sent, "mine")
    each(sent, "twist")
    each(sent_here, "pair")
    energy_sent(0)
    energy_sent(1)
    energy_sent(5)

    @pl.when(has_down)
    def _():
        each(sent_here, "below")
        energy_sent(2)

    @pl.when(has_up)
    def _():
        each(sent_up, "above")
        each(sent_up, "other")
        energy_sent(3)
        energy_sent(4)

    pl.when(has_both)(lambda: each(sent_up, "span"))


def on_device(n_chan, n_win, spectra, near):
    _, freqs, depth, width = spectra.shape
    rounds = near.shape[1] + 1
    rows, n_y = width // n_win, n_win // 2
    bf, f32 = jnp.bfloat16, jnp.float32
    dma = pltpu.SemaphoreType.DMA
    out = pl.pallas_call(
        functools.partial(kernel, n_chan, n_win, float(depth * n_win)),
        out_shape=jax.ShapeDtypeStruct((rows * rounds * 2 * freqs * (width // 128), 128), f32),
        in_specs=[pl.BlockSpec(memory_space=pltpu.VMEM), pl.BlockSpec(memory_space=pltpu.SMEM)],
        out_specs=pl.BlockSpec(memory_space=pltpu.VMEM),
        scratch_shapes=[
            pltpu.VMEM((6, 2, depth, width), bf),
            pltpu.VMEM((5, 2 * width, 2 * depth), bf),
            pltpu.VMEM((8, width, width), f32),
            pltpu.VMEM((8, width, width), bf),
            pltpu.VMEM((8, width, width), bf),
            pltpu.VMEM((8, n_y - 1, 2 * rows, width), bf),
            pltpu.VMEM((8, n_y - 1, 2 * rows, width), bf),
            pltpu.VMEM((8, 2, rows, width), bf),
            pltpu.VMEM((rounds, 2, 2, rows, width), bf),
            pltpu.VMEM((6, 8, width), f32),
            pltpu.VMEM((6, n_win - 1, 8, width), f32),
            pltpu.VMEM((6, 8, width), f32),
            pltpu.VMEM((5, rows, 128), f32),
            dma((2,)), dma((2,)), dma((2,)), dma((2,)), dma((2,)), dma((2,)), dma((8,)), dma((8,)),
            dma((8, n_y - 1)), dma((8, n_y - 1)), dma((8,)), dma((rounds, 2)),
            dma((6, n_win - 1)), dma((6, n_win - 1)),
        ],
        compiler_params=pltpu.CompilerParams(
            collective_id=0, has_side_effects=True, vmem_limit_bytes=56 * 1024 * 1024),
        cost_estimate=pl.CostEstimate(
            flops=64 * depth * width * width, bytes_accessed=6 * 1024 * 1024, transcendentals=0),
    )(spectra, near)
    out = out.reshape(rows, rounds, 2, width // 128, freqs, 128)
    return jnp.transpose(out, (0, 1, 2, 4, 3, 5)).reshape(rows, rounds, 2, freqs, width)


def solution(mesh):
    sizes = dict(mesh.shape)
    return jax.shard_map(
        functools.partial(on_device, sizes["chan"], sizes["win"]),
        mesh=mesh,
        in_specs=(P(None, None, "win", "chan"), P("chan", None)),
        out_specs=P(("chan", "win"), None, None, None, None),
        check_vma=False,
    )
```

```python
import functools

import jax
import jax.numpy as jnp
from jax import lax
from jax.experimental import pallas as pl
from jax.experimental.pallas import tpu as pltpu
from jax.sharding import PartitionSpec as P

MESH = pl.DeviceIdType.MESH
LIFT = 2.0**40
EPS = 1e-06


def kernel(n_chan, n_win, windows, x_ref, near_ref, result_ref, out_ref, blk, left, own, cs, cr, ys, yr, xs, xr,
           es, er, scale, column, bx_s, bx_r, bu_s, bu_r, bd_s, bd_r, c_s, c_r, y_s, y_r, r_s, r_r,
           e_s, e_r, in_s, out_s):
    depth, width = x_ref.shape[2], x_ref.shape[3]
    rows = width // n_win
    n_y = n_win // 2
    rounds, step_rows = result_ref.shape[1], result_ref.shape[1] * result_ref.shape[2]
    flat = out_ref.reshape(rows * step_rows, 128)
    chan, win = lax.axis_index("chan"), lax.axis_index("win")
    p, pair = lax.rem(chan, 2), chan // 2
    core, y = lax.rem(win, 2), win // 2
    has_up = pair < n_chan // 2 - 1
    has_down = pair >= 1
    has_both = jnp.logical_and(has_up, has_down)
    even, odd = p == 0, p == 1
    mate = (chan + 1 - 2 * p, win)
    up, down = (chan + 2, win), (chan - 2, win)
    up_mate, down_mate = (chan + 3 - 2 * p, win), (chan - 1 - 2 * p, win)
    twin = (chan, win + 1 - 2 * core)

    def win_peer(d):
        return (chan, lax.rem(win + d, n_win))

    def y_peer(d):
        return lax.rem(y + d, n_y)

    def remote(src, dst, ss, rs, to):
        return pltpu.make_async_remote_copy(
            src_ref=src, dst_ref=dst, send_sem=ss, recv_sem=rs, device_id=to, device_id_type=MESH)

    def exchange(c):
        return remote(x_ref.at[c, 1 - p], blk.at[p, c], bx_s.at[c], bx_r.at[c], mate)

    def exchanged(c):
        return remote(x_ref.at[c, p], blk.at[1 - p, c], bx_s.at[c], bx_r.at[c], mate)

    def climb(c):
        return remote(blk.at[1, c], blk.at[2, c], bu_s.at[c], bu_r.at[c], up)

    def climb_own(c):
        return remote(x_ref.at[c, p], blk.at[2, c], bu_s.at[c], bu_r.at[c], up)

    def descend_own():
        return remote(x_ref.at[:, p], blk.at[3 + p], bd_s.at[0], bd_r.at[0], down)

    def descend_other():
        return remote(blk.at[1 - p], blk.at[4 - p], bd_s.at[1], bd_r.at[1], down)

    def load(n, f, slot):
        return pltpu.make_async_copy(x_ref.at[:, f], blk.at[slot], in_s.at[n])

    def core_copy(k):
        return remote(cs.at[k], cr.at[k], c_s.at[k], c_r.at[k], twin)

    def y_copy(k, d):
        return remote(ys.at[k, d - 1], yr.at[k, d - 1], y_s.at[k, d - 1], y_r.at[k, d - 1],
                      (chan, y_peer(d) * 2 + core))

    def result_copy(m, r, w, to):
        return remote(xs.at[m], xr.at[r, w], r_s.at[m], r_r.at[r, w], to)

    def energy_copy(s, d):
        return remote(es.at[s], er.at[s, d - 1], e_s.at[s, d - 1], e_r.at[s, d - 1], win_peer(d))

    load(0, p, p).start()
    load(1, 1 - p, 5).start()
    barrier = pltpu.get_barrier_semaphore()

    def greet(*others):
        for to in others:
            pl.semaphore_signal(barrier, inc=1, device_id=to, device_id_type=MESH)

    greet(mate)
    for d in range(1, n_win):
        greet(win_peer(d))
    pl.when(has_up)(lambda: greet(up, up_mate))
    pl.when(has_down)(lambda: greet(down, down_mate))
    pl.semaphore_wait(barrier, n_win + 2 * (has_up.astype(jnp.int32) + has_down.astype(jnp.int32)))

    for c in range(2):
        exchange(c).start()

    @pl.when(has_down)
    def _():
        descend_own().start()

    @pl.when(jnp.logical_and(has_up, odd))
    def _():
        for c in range(2):
            climb_own(c).start()

    def energy(s):
        def step(i, total):
            part = blk[s, :, pl.ds(pl.multiple_of(i * 64, 64), 64)].astype(jnp.float32)
            return total + jnp.sum((part * part).reshape(2 * 8, 8, width), axis=0)

        total = lax.fori_loop(0, depth // 64, step, jnp.zeros((8, width), jnp.float32))
        es[s] = jnp.broadcast_to(jnp.sum(total, axis=0, keepdims=True), (8, width))
        for d in range(1, n_win):
            energy_copy(s, d).start()

    def finish_energy(s):
        total = es[s]
        for d in range(1, n_win):
            energy_copy(s, d).wait_recv()
            total = total + er[s, d - 1]
        scale[s] = lax.rsqrt(total / windows + EPS)

    def finish_column(kb, s):
        row = lax.broadcasted_iota(jnp.int32, (rows, width), 0) + win * rows
        lane = lax.broadcasted_iota(jnp.int32, (rows, width), 1)
        wide = jnp.broadcast_to(scale[s, 0:1], (rows, width))
        picked = jnp.sum(jnp.where(row == lane, wide, 0.0), axis=1, keepdims=True)
        column[kb] = jnp.broadcast_to(picked * (1.0 / LIFT), (rows, 128))

    def build_left(kb, s):
        lift = jnp.asarray(LIFT, jnp.bfloat16)
        real = (blk[s, 0] * lift).T
        imag = (blk[s, 1] * lift).T
        for q in range(n_win):
            base = ((q % 2) * n_y + q // 2) * 2 * rows
            cut = slice(q * rows, (q + 1) * rows)
            left[kb, base:base + rows, :depth] = real[cut]
            left[kb, base:base + rows, depth:] = imag[cut]
            left[kb, base + rows:base + 2 * rows, :depth] = -imag[cut]
            left[kb, base + rows:base + 2 * rows, depth:] = real[cut]

    def product(m, kb, s, q, r):
        right = blk[s].reshape(2 * depth, width)
        far = pl.multiple_of((1 - core) * width, width)
        near_by = pl.multiple_of(core * width, width)
        cs[m] = jnp.dot(left[kb, pl.ds(far, width)], right, preferred_element_type=jnp.float32).astype(jnp.bfloat16)
        core_copy(m).start()
        own[m] = jnp.dot(left[kb, pl.ds(near_by, width)], right, preferred_element_type=jnp.float32)

    def fold(m, kb, s, q, r):
        core_copy(m).wait_recv()
        for d in range(1, n_y):
            cut = pl.ds(pl.multiple_of(y_peer(d) * 2 * rows, 2 * rows), 2 * rows)
            ys[m, d - 1] = (own[m, cut] + cr[m, cut].astype(jnp.float32)).astype(jnp.bfloat16)
            y_copy(m, d).start()

    def weight(r):
        value = near_ref[0, jnp.maximum(r - 1, 0)]
        return jnp.where(r == 0, 1.0, value.astype(jnp.float32))

    def store(r, f, value):
        value = value * weight(r)
        for c in range(2):
            for tile in range(width // 128):
                at = pl.ds(((r * 2 + c) * (width // 128) + tile) * 2 + f, rows, stride=step_rows)
                flat[at, :] = value[c, :, tile * 128:(tile + 1) * 128]

    def total_of(m, kb, s):
        cut = pl.ds(pl.multiple_of(y * 2 * rows, 2 * rows), 2 * rows)
        total = own[m, cut] + cr[m, cut].astype(jnp.float32)
        for d in range(1, n_y):
            y_copy(m, d).wait_recv()
            total = total + yr[m, d - 1].astype(jnp.float32)
        return total.reshape(2, rows, width) * (column[kb][:, 0:1] * scale[s, 0:1])[None]

    def final_here(m, kb, s, q, r):
        total = total_of(m, kb, s)

        @pl.when(q == p)
        def _():
            store(r, p, total)

        @pl.when(q != p)
        def _():
            xs[m] = total.astype(jnp.bfloat16)
            result_copy(m, r, 0, mate).start()

    def final_twist(m, kb, s, q, r):
        store(r, 1 - p, total_of(m, kb, s))

    def target_up(m, r, q):
        same = (q == p).astype(jnp.int32)
        return result_copy(m, r, same, (chan - p + 2 + q, win))

    def final_up(m, kb, s, q, r):
        xs[m] = total_of(m, kb, s).astype(jnp.bfloat16)
        target_up(m, r, q).start()

    groups = dict(
        mine=(1, lambda n: (0 * n, p, p, p, 0 * n)),
        twist=(1, lambda n: (0 * n + 1, 0 * n + 4, 0 * n + 5, p, 0 * n)),
        pair=(1, lambda n: (0 * n + 2, 0 * n + 1, 0 * n, 0 * n + 1, 0 * n + 1)),
        above=(1, lambda n: (5 + p + 0 * n, 2 + p, 0 * n, p, 2 + p)),
        below=(2, lambda n: (3 + n, n, 0 * n + 2, n, 1 + n)),
        other=(1, lambda n: (6 - p + 0 * n, 3 - p, 0 * n, 1 - p, 3 - p)),
        span=(1, lambda n: (0 * n + 7, 0 * n + 2, 0 * n + 2, 0 * n, 0 * n + 3)),
    )

    def each(work, g):
        count, params = groups[g]

        def step(n, carry):
            work(*params(n))
            return carry

        lax.fori_loop(0, count, step, 0)

    def make(g):
        each(product, g)
        each(fold, g)

    load(0, p, p).wait()
    build_left(p, p)
    each(product, "mine")
    load(1, 1 - p, 5).wait()
    build_left(4, 5)
    each(product, "twist")
    each(fold, "mine")
    each(fold, "twist")
    energy(p)
    energy(5)
    for c in range(2):
        exchanged(c).wait_recv()
        pl.when(jnp.logical_and(has_up, even))(lambda: climb(c).start())
    pl.when(has_down)(lambda: descend_other().start())
    build_left(1 - p, 1 - p)
    make("pair")
    energy(1 - p)

    @pl.when(has_up)
    def _():
        descend_own().wait_recv()
        build_left(2 + p, 3 + p)
        make("above")
        energy(3 + p)

    for s in range(2):
        finish_energy(s)
        finish_column(s, s)
    finish_energy(5)
    finish_column(4, 5)
    each(final_here, "mine")
    each(final_twist, "twist")

    @pl.when(has_down)
    def _():
        for c in range(2):
            climb(c).wait_recv()
        make("below")
        energy(2)

    pl.when(jnp.logical_and(has_both, even))(lambda: make("span"))
    each(final_here, "pair")

    @pl.when(has_up)
    def _():
        finish_energy(3 + p)
        finish_column(2 + p, 3 + p)
        each(final_up, "above")
        descend_other().wait_recv()
        build_left(3 - p, 4 - p)
        make("other")
        energy(4 - p)

    pl.when(jnp.logical_and(has_both, odd))(lambda: make("span"))

    @pl.when(has_down)
    def _():
        finish_energy(2)
        each(final_here, "below")

    pl.when(jnp.logical_and(has_both, even))(lambda: each(final_up, "span"))

    @pl.when(has_up)
    def _():
        finish_energy(4 - p)
        finish_column(3 - p, 4 - p)
        each(final_up, "other")

    pl.when(jnp.logical_and(has_both, odd))(lambda: each(final_up, "span"))

    def written(r):
        return pltpu.make_async_copy(out_ref.at[:, r], result_ref.at[:, r], out_s.at[r])

    def receive(r, carry):
        @pl.when(jnp.logical_and(chan >= r, r >= 1))
        def _():
            result_copy(0, r, 0, mate).wait_recv()
            store(r, 1 - p, xr[r, 0].astype(jnp.float32).reshape(2, rows, width))

        @pl.when(jnp.logical_and(chan >= r, r >= 2 + p))
        def _():
            result_copy(0, r, 1, mate).wait_recv()
            store(r, p, xr[r, 1].astype(jnp.float32).reshape(2, rows, width))

        @pl.when(chan < r)
        def _():
            for f in range(2):
                store(r, f, jnp.zeros((2, rows, width), jnp.float32))

        written(r).start()
        return carry

    lax.fori_loop(0, 4, receive, 0)

    for c in range(2):
        exchange(c).wait_send()

    @pl.when(has_up)
    def _():
        for c in range(2):
            climb(c).wait_send()

    @pl.when(has_down)
    def _():
        descend_own().wait_send()
        descend_other().wait_send()

    def sent(m, kb, s, q, r):
        core_copy(m).wait_send()
        for d in range(1, n_y):
            y_copy(m, d).wait_send()

    def sent_here(m, kb, s, q, r):
        sent(m, kb, s, q, r)
        pl.when(q != p)(lambda: result_copy(m, r, 0, mate).wait_send())

    def sent_up(m, kb, s, q, r):
        sent(m, kb, s, q, r)
        target_up(m, r, q).wait_send()

    def energy_sent(s):
        for d in range(1, n_win):
            energy_copy(s, d).wait_send()

    each(sent, "mine")
    each(sent, "twist")
    each(sent_here, "pair")
    energy_sent(0)
    energy_sent(1)
    energy_sent(5)

    @pl.when(has_down)
    def _():
        each(sent_here, "below")
        energy_sent(2)

    @pl.when(has_up)
    def _():
        each(sent_up, "above")
        each(sent_up, "other")
        energy_sent(3)
        energy_sent(4)

    pl.when(has_both)(lambda: each(sent_up, "span"))
    for r in range(rounds):
        written(r).wait()


def on_device(n_chan, n_win, spectra, near):
    _, freqs, depth, width = spectra.shape
    rounds = near.shape[1] + 1
    rows, n_y = width // n_win, n_win // 2
    bf, f32 = jnp.bfloat16, jnp.float32
    out_shape = (rows, rounds, 2 * freqs * (width // 128), 128)
    dma = pltpu.SemaphoreType.DMA
    out = pl.pallas_call(
        functools.partial(kernel, n_chan, n_win, float(depth * n_win)),
        out_shape=jax.ShapeDtypeStruct(out_shape, f32),
        in_specs=[pl.BlockSpec(memory_space=pl.ANY), pl.BlockSpec(memory_space=pltpu.SMEM)],
        out_specs=pl.BlockSpec(memory_space=pl.ANY),
        scratch_shapes=[
            pltpu.VMEM(out_shape, f32),
            pltpu.VMEM((6, 2, depth, width), bf),
            pltpu.VMEM((5, 2 * width, 2 * depth), bf),
            pltpu.VMEM((8, width, width), f32),
            pltpu.VMEM((8, width, width), bf),
            pltpu.VMEM((8, width, width), bf),
            pltpu.VMEM((8, n_y - 1, 2 * rows, width), bf),
            pltpu.VMEM((8, n_y - 1, 2 * rows, width), bf),
            pltpu.VMEM((8, 2, rows, width), bf),
            pltpu.VMEM((rounds, 2, 2, rows, width), bf),
            pltpu.VMEM((6, 8, width), f32),
            pltpu.VMEM((6, n_win - 1, 8, width), f32),
            pltpu.VMEM((6, 8, width), f32),
            pltpu.VMEM((5, rows, 128), f32),
            dma((2,)), dma((2,)), dma((2,)), dma((2,)), dma((2,)), dma((2,)), dma((8,)), dma((8,)),
            dma((8, n_y - 1)), dma((8, n_y - 1)), dma((8,)), dma((rounds, 2)),
            dma((6, n_win - 1)), dma((6, n_win - 1)), dma((2,)), dma((rounds,)),
        ],
        compiler_params=pltpu.CompilerParams(
            collective_id=0, has_side_effects=True, vmem_limit_bytes=56 * 1024 * 1024),
        cost_estimate=pl.CostEstimate(
            flops=64 * depth * width * width, bytes_accessed=6 * 1024 * 1024, transcendentals=0),
    )(spectra, near)
    out = (out * (1.0 / (depth * n_win))).reshape(rows, rounds, 2, width // 128, freqs, 128)
    return jnp.transpose(out, (0, 1, 2, 4, 3, 5)).reshape(rows, rounds, 2, freqs, width)


def solution(mesh):
    sizes = dict(mesh.shape)
    return jax.shard_map(
        functools.partial(on_device, sizes["chan"], sizes["win"]),
        mesh=mesh,
        in_specs=(P(None, None, "win", "chan"), P("chan", None)),
        out_specs=P(("chan", "win"), None, None, None, None),
        check_vma=False,
    )
```

```python
import functools

import jax
import jax.numpy as jnp
from jax import lax
from jax.experimental import pallas as pl
from jax.experimental.pallas import tpu as pltpu
from jax.sharding import PartitionSpec as P

MESH = pl.DeviceIdType.MESH
LIFT = 2.0**40
EPS = 1e-06


def kernel(n_chan, n_win, windows, x_ref, near_ref, result_ref, out_ref, blk, left, own, cs, cr, ys, yr, xs, xr,
           es, er, scale, column, bx_s, bx_r, bu_s, bu_r, bd_s, bd_r, c_s, c_r, y_s, y_r, r_s, r_r,
           e_s, e_r, in_s, out_s):
    depth, width = x_ref.shape[2], x_ref.shape[3]
    rows = width // n_win
    n_y = n_win // 2
    rounds, step_rows = result_ref.shape[1], result_ref.shape[1] * result_ref.shape[2]
    flat = out_ref.reshape(rows * step_rows, 128)
    chan, win = lax.axis_index("chan"), lax.axis_index("win")
    p, pair = lax.rem(chan, 2), chan // 2
    core, y = lax.rem(win, 2), win // 2
    has_up = pair < n_chan // 2 - 1
    has_down = pair >= 1
    has_both = jnp.logical_and(has_up, has_down)
    even, odd = p == 0, p == 1
    mate = (chan + 1 - 2 * p, win)
    up, down = (chan + 2, win), (chan - 2, win)
    up_mate, down_mate = (chan + 3 - 2 * p, win), (chan - 1 - 2 * p, win)
    twin = (chan, win + 1 - 2 * core)

    def win_peer(d):
        return (chan, lax.rem(win + d, n_win))

    def y_peer(d):
        return lax.rem(y + d, n_y)

    def remote(src, dst, ss, rs, to):
        return pltpu.make_async_remote_copy(
            src_ref=src, dst_ref=dst, send_sem=ss, recv_sem=rs, device_id=to, device_id_type=MESH)

    def exchange(c):
        return remote(x_ref.at[c, 1 - p], blk.at[p, c], bx_s.at[c], bx_r.at[c], mate)

    def exchanged(c):
        return remote(x_ref.at[c, p], blk.at[1 - p, c], bx_s.at[c], bx_r.at[c], mate)

    def climb(c):
        return remote(blk.at[1, c], blk.at[2, c], bu_s.at[c], bu_r.at[c], up)

    def climb_own(c):
        return remote(x_ref.at[c, p], blk.at[2, c], bu_s.at[c], bu_r.at[c], up)

    def descend_own():
        return remote(x_ref.at[:, p], blk.at[3 + p], bd_s.at[0], bd_r.at[0], down)

    def descend_other():
        return remote(blk.at[1 - p], blk.at[4 - p], bd_s.at[1], bd_r.at[1], down)

    def load(n, f, slot):
        return pltpu.make_async_copy(x_ref.at[:, f], blk.at[slot], in_s.at[n])

    def core_copy(k):
        return remote(cs.at[k], cr.at[k], c_s.at[k], c_r.at[k], twin)

    def y_copy(k, d):
        return remote(ys.at[k, d - 1], yr.at[k, d - 1], y_s.at[k, d - 1], y_r.at[k, d - 1],
                      (chan, y_peer(d) * 2 + core))

    def result_copy(m, r, w, to):
        return remote(xs.at[m], xr.at[r, w], r_s.at[m], r_r.at[r, w], to)

    def energy_copy(s, d):
        return remote(es.at[s], er.at[s, d - 1], e_s.at[s, d - 1], e_r.at[s, d - 1], win_peer(d))

    load(0, p, p).start()
    load(1, 1 - p, 5).start()
    barrier = pltpu.get_barrier_semaphore()

    def greet(*others):
        for to in others:
            pl.semaphore_signal(barrier, inc=1, device_id=to, device_id_type=MESH)

    greet(mate)
    for d in range(1, n_win):
        greet(win_peer(d))
    pl.when(has_up)(lambda: greet(up, up_mate))
    pl.when(has_down)(lambda: greet(down, down_mate))
    pl.semaphore_wait(barrier, n_win + 2 * (has_up.astype(jnp.int32) + has_down.astype(jnp.int32)))

    for c in range(2):
        exchange(c).start()

    @pl.when(has_down)
    def _():
        descend_own().start()

    @pl.when(jnp.logical_and(has_up, odd))
    def _():
        for c in range(2):
            climb_own(c).start()

    def energy(s):
        def step(i, total):
            part = blk[s, :, pl.ds(pl.multiple_of(i * 64, 64), 64)].astype(jnp.float32)
            return total + jnp.sum((part * part).reshape(2 * 8, 8, width), axis=0)

        total = lax.fori_loop(0, depth // 64, step, jnp.zeros((8, width), jnp.float32))
        es[s] = jnp.sum(total, axis=0, keepdims=True)
        for d in range(1, n_win):
            energy_copy(s, d).start()

    def finish_energy(s):
        total = es[s]
        for d in range(1, n_win):
            energy_copy(s, d).wait_recv()
            total = total + er[s, d - 1]
        scale[s] = jnp.broadcast_to(lax.rsqrt(total / windows + EPS), (8, width))

    def finish_column(kb, s):
        row = lax.broadcasted_iota(jnp.int32, (rows, width), 0) + win * rows
        lane = lax.broadcasted_iota(jnp.int32, (rows, width), 1)
        wide = jnp.broadcast_to(scale[s, 0:1], (rows, width))
        picked = jnp.sum(jnp.where(row == lane, wide, 0.0), axis=1, keepdims=True)
        column[kb] = jnp.broadcast_to(picked * (1.0 / LIFT), (rows, 128))

    def build_left(kb, s):
        lift = jnp.asarray(LIFT, jnp.bfloat16)
        real = (blk[s, 0] * lift).T
        imag = (blk[s, 1] * lift).T
        for q in range(n_win):
            base = ((q % 2) * n_y + q // 2) * 2 * rows
            cut = slice(q * rows, (q + 1) * rows)
            left[kb, base:base + rows, :depth] = real[cut]
            left[kb, base:base + rows, depth:] = imag[cut]
            left[kb, base + rows:base + 2 * rows, :depth] = -imag[cut]
            left[kb, base + rows:base + 2 * rows, depth:] = real[cut]

    def product(m, kb, s, q, r):
        right = blk[s].reshape(2 * depth, width)
        far = pl.multiple_of((1 - core) * width, width)
        near_by = pl.multiple_of(core * width, width)
        cs[m] = jnp.dot(left[kb, pl.ds(far, width)], right, preferred_element_type=jnp.float32).astype(jnp.bfloat16)
        core_copy(m).start()
        own[m] = jnp.dot(left[kb, pl.ds(near_by, width)], right, preferred_element_type=jnp.float32)

    def fold(m, kb, s, q, r):
        core_copy(m).wait_recv()
        for d in range(1, n_y):
            cut = pl.ds(pl.multiple_of(y_peer(d) * 2 * rows, 2 * rows), 2 * rows)
            ys[m, d - 1] = (own[m, cut] + cr[m, cut].astype(jnp.float32)).astype(jnp.bfloat16)
            y_copy(m, d).start()

    def weight(r):
        value = near_ref[0, jnp.maximum(r - 1, 0)]
        return jnp.where(r == 0, 1.0, value.astype(jnp.float32))

    def store(r, f, value):
        value = value * weight(r)
        for c in range(2):
            for tile in range(width // 128):
                at = pl.ds(((r * 2 + c) * (width // 128) + tile) * 2 + f, rows, stride=step_rows)
                flat[at, :] = value[c, :, tile * 128:(tile + 1) * 128]

    def total_of(m, kb, s):
        cut = pl.ds(pl.multiple_of(y * 2 * rows, 2 * rows), 2 * rows)
        total = own[m, cut] + cr[m, cut].astype(jnp.float32)
        for d in range(1, n_y):
            y_copy(m, d).wait_recv()
            total = total + yr[m, d - 1].astype(jnp.float32)
        return total.reshape(2, rows, width) * (column[kb][:, 0:1] * scale[s, 0:1])[None]

    def final_here(m, kb, s, q, r):
        total = total_of(m, kb, s)

        @pl.when(q == p)
        def _():
            store(r, p, total)

        @pl.when(q != p)
        def _():
            xs[m] = total.astype(jnp.bfloat16)
            result_copy(m, r, 0, mate).start()

    def final_twist(m, kb, s, q, r):
        store(r, 1 - p, total_of(m, kb, s))

    def target_up(m, r, q):
        same = (q == p).astype(jnp.int32)
        return result_copy(m, r, same, (chan - p + 2 + q, win))

    def final_up(m, kb, s, q, r):
        xs[m] = total_of(m, kb, s).astype(jnp.bfloat16)
        target_up(m, r, q).start()

    groups = dict(
        mine=(1, lambda n: (0 * n, p, p, p, 0 * n)),
        twist=(1, lambda n: (0 * n + 1, 0 * n + 4, 0 * n + 5, p, 0 * n)),
        pair=(1, lambda n: (0 * n + 2, 0 * n + 1, 0 * n, 0 * n + 1, 0 * n + 1)),
        above=(1, lambda n: (5 + p + 0 * n, 2 + p, 0 * n, p, 2 + p)),
        below=(2, lambda n: (3 + n, n, 0 * n + 2, n, 1 + n)),
        other=(1, lambda n: (6 - p + 0 * n, 3 - p, 0 * n, 1 - p, 3 - p)),
        span=(1, lambda n: (0 * n + 7, 0 * n + 2, 0 * n + 2, 0 * n, 0 * n + 3)),
    )

    def each(work, g):
        count, params = groups[g]

        def step(n, carry):
            work(*params(n))
            return carry

        lax.fori_loop(0, count, step, 0)

    def make(g):
        each(product, g)
        each(fold, g)

    load(0, p, p).wait()
    build_left(p, p)
    each(product, "mine")
    load(1, 1 - p, 5).wait()
    build_left(4, 5)
    each(product, "twist")
    each(fold, "mine")
    each(fold, "twist")
    energy(p)
    energy(5)
    for c in range(2):
        exchanged(c).wait_recv()
        pl.when(jnp.logical_and(has_up, even))(lambda: climb(c).start())
    pl.when(has_down)(lambda: descend_other().start())
    build_left(1 - p, 1 - p)
    make("pair")
    energy(1 - p)

    @pl.when(has_up)
    def _():
        descend_own().wait_recv()
        build_left(2 + p, 3 + p)
        make("above")
        energy(3 + p)

    for s in range(2):
        finish_energy(s)
        finish_column(s, s)
    finish_energy(5)
    finish_column(4, 5)
    each(final_here, "mine")
    each(final_twist, "twist")

    @pl.when(has_down)
    def _():
        for c in range(2):
            climb(c).wait_recv()
        make("below")
        energy(2)

    pl.when(jnp.logical_and(has_both, even))(lambda: make("span"))
    each(final_here, "pair")

    @pl.when(has_up)
    def _():
        finish_energy(3 + p)
        finish_column(2 + p, 3 + p)
        each(final_up, "above")
        descend_other().wait_recv()
        build_left(3 - p, 4 - p)
        make("other")
        energy(4 - p)

    pl.when(jnp.logical_and(has_both, odd))(lambda: make("span"))

    @pl.when(has_down)
    def _():
        finish_energy(2)
        each(final_here, "below")

    pl.when(jnp.logical_and(has_both, even))(lambda: each(final_up, "span"))

    @pl.when(has_up)
    def _():
        finish_energy(4 - p)
        finish_column(3 - p, 4 - p)
        each(final_up, "other")

    pl.when(jnp.logical_and(has_both, odd))(lambda: each(final_up, "span"))

    def written(r):
        return pltpu.make_async_copy(out_ref.at[:, r], result_ref.at[:, r], out_s.at[r])

    def receive(r, carry):
        @pl.when(jnp.logical_and(chan >= r, r >= 1))
        def _():
            result_copy(0, r, 0, mate).wait_recv()
            store(r, 1 - p, xr[r, 0].astype(jnp.float32).reshape(2, rows, width))

        @pl.when(jnp.logical_and(chan >= r, r >= 2 + p))
        def _():
            result_copy(0, r, 1, mate).wait_recv()
            store(r, p, xr[r, 1].astype(jnp.float32).reshape(2, rows, width))

        @pl.when(chan < r)
        def _():
            for f in range(2):
                store(r, f, jnp.zeros((2, rows, width), jnp.float32))

        written(r).start()
        return carry

    lax.fori_loop(0, 4, receive, 0)

    for c in range(2):
        exchange(c).wait_send()

    @pl.when(has_up)
    def _():
        for c in range(2):
            climb(c).wait_send()

    @pl.when(has_down)
    def _():
        descend_own().wait_send()
        descend_other().wait_send()

    def sent(m, kb, s, q, r):
        core_copy(m).wait_send()
        for d in range(1, n_y):
            y_copy(m, d).wait_send()

    def sent_here(m, kb, s, q, r):
        sent(m, kb, s, q, r)
        pl.when(q != p)(lambda: result_copy(m, r, 0, mate).wait_send())

    def sent_up(m, kb, s, q, r):
        sent(m, kb, s, q, r)
        target_up(m, r, q).wait_send()

    def energy_sent(s):
        for d in range(1, n_win):
            energy_copy(s, d).wait_send()

    each(sent, "mine")
    each(sent, "twist")
    each(sent_here, "pair")
    energy_sent(0)
    energy_sent(1)
    energy_sent(5)

    @pl.when(has_down)
    def _():
        each(sent_here, "below")
        energy_sent(2)

    @pl.when(has_up)
    def _():
        each(sent_up, "above")
        each(sent_up, "other")
        energy_sent(3)
        energy_sent(4)

    pl.when(has_both)(lambda: each(sent_up, "span"))
    for r in range(rounds):
        written(r).wait()


def on_device(n_chan, n_win, spectra, near):
    _, freqs, depth, width = spectra.shape
    rounds = near.shape[1] + 1
    rows, n_y = width // n_win, n_win // 2
    bf, f32 = jnp.bfloat16, jnp.float32
    out_shape = (rows, rounds, 2 * freqs * (width // 128), 128)
    dma = pltpu.SemaphoreType.DMA
    out = pl.pallas_call(
        functools.partial(kernel, n_chan, n_win, float(depth * n_win)),
        out_shape=jax.ShapeDtypeStruct(out_shape, f32),
        in_specs=[pl.BlockSpec(memory_space=pl.ANY), pl.BlockSpec(memory_space=pltpu.SMEM)],
        out_specs=pl.BlockSpec(memory_space=pl.ANY),
        scratch_shapes=[
            pltpu.VMEM(out_shape, f32),
            pltpu.VMEM((6, 2, depth, width), bf),
            pltpu.VMEM((5, 2 * width, 2 * depth), bf),
            pltpu.VMEM((8, width, width), f32),
            pltpu.VMEM((8, width, width), bf),
            pltpu.VMEM((8, width, width), bf),
            pltpu.VMEM((8, n_y - 1, 2 * rows, width), bf),
            pltpu.VMEM((8, n_y - 1, 2 * rows, width), bf),
            pltpu.VMEM((8, 2, rows, width), bf),
            pltpu.VMEM((rounds, 2, 2, rows, width), bf),
            pltpu.VMEM((6, 1, width), f32),
            pltpu.VMEM((6, n_win - 1, 1, width), f32),
            pltpu.VMEM((6, 8, width), f32),
            pltpu.VMEM((5, rows, 128), f32),
            dma((2,)), dma((2,)), dma((2,)), dma((2,)), dma((2,)), dma((2,)), dma((8,)), dma((8,)),
            dma((8, n_y - 1)), dma((8, n_y - 1)), dma((8,)), dma((rounds, 2)),
            dma((6, n_win - 1)), dma((6, n_win - 1)), dma((2,)), dma((rounds,)),
        ],
        compiler_params=pltpu.CompilerParams(
            collective_id=0, has_side_effects=True, vmem_limit_bytes=56 * 1024 * 1024),
        cost_estimate=pl.CostEstimate(
            flops=64 * depth * width * width, bytes_accessed=6 * 1024 * 1024, transcendentals=0),
    )(spectra, near)
    out = (out * (1.0 / (depth * n_win))).reshape(rows, rounds, 2, width // 128, freqs, 128)
    return jnp.transpose(out, (0, 1, 2, 4, 3, 5)).reshape(rows, rounds, 2, freqs, width)


def solution(mesh):
    sizes = dict(mesh.shape)
    return jax.shard_map(
        functools.partial(on_device, sizes["chan"], sizes["win"]),
        mesh=mesh,
        in_specs=(P(None, None, "win", "chan"), P("chan", None)),
        out_specs=P(("chan", "win"), None, None, None, None),
        check_vma=False,
    )
```
